256 devices in a mesh: section: 32 (over x, z), dp: 8 (over y, core).
Axes of the slice: x: 4, y: 4, z: 8, core: 2. Of those that a mesh axis runs over, the one named last changes fastest.
Arguments:
- hidden: bfloat16 [512, 4608], P('dp', 'section'), may hold values from -6 to 6
- norm_gain: float32 [4608], replicated, may hold values from -0.5 to 0.5
- weight: bfloat16 [256000, 4608], P(('section', 'dp'))
- targets: int32 [8, 64], replicated, may hold values from 0 to 255999
- segment_ids: int32 [8, 64], replicated, may hold values from 0 to 7, never falling along the last dimension, each value on 1 to 16 neighbouring positions
- pairing: int32 [8, 8], replicated, may hold values from 0 to 7, each once within a row
- ref_logp: float32 [8, 8], replicated, may hold values from -30 to -20
Outputs:
- hidden_grad: float32 [512, 4608], P('dp', 'section')
- margins: float32 [8, 4], P('dp')
- dpo_loss: float32 [], replicated
The draws below stay inside these ranges and needn't reach their ends.
Inputs may be any that keep to these rules, and one draw needn't show every extreme that they name: `segment_ids`: within each group's row the segment ids never fall and every one of the 8 segments holds at least one token; one segment of each row holds exactly 16. `pairing`: each row holds every segment number once.
All inputs are finite; a program needn't handle non-finite values.
Results may differ from the reference program's by a relative error of at most 0.0046.
Values may be sent and summed in bfloat16 or wider, within the bound.
A program may use at most 128 MiB of HBM per device.

```python
import math
import jax
import jax.numpy as jnp
import numpy as np
from jax import lax

D = 4608
V_DEV = 1000
TOK_GRP = 64
SEGS = 8
TOKENS = 512
V = 256000
N_DP = 8


def draw_weight(key, part):
    key = jax.random.fold_in(key, 11)
    entry_key, scale_key = jax.random.split(key, 2)
    entries = jax.random.normal(entry_key, (V, D), jnp.float32)
    spread = math.log(4.0)
    row_index = jnp.arange(V, dtype=jnp.float32)
    rise = 1.0 + 2.0 * row_index / V
    row_scale = jnp.exp(jax.random.uniform(scale_key, (V, 1), jnp.float32, 0.0, spread)) * rise[:, None]
    return (entries * row_scale * (1.0 / math.sqrt(D))).astype(jnp.bfloat16)


def touch_ends(drawn, own_key, low, top_value):
    place = [jax.random.randint(jax.random.fold_in(own_key, axis), (), 0, length) for axis, length in enumerate(drawn.shape)]
    main_axis = drawn.shape.index(max(drawn.shape))
    neighbour = place[:main_axis] + [(place[main_axis] + 1) % drawn.shape[main_axis]] + place[main_axis + 1:]
    return drawn.at[tuple(place)].set(low).at[tuple(neighbour)].set(top_value)


def steps_of(rng, extent, pieces, low, top_value):
    def one(axis_at, blocks):
        heights = jax.random.uniform(jax.random.fold_in(jax.random.fold_in(rng, 6), axis_at), (blocks,), jnp.float32, low / len(pieces), top_value / len(pieces))
        return jnp.repeat(jnp.exp(heights), extent[axis_at] // blocks).reshape((-1,) + (1,) * (len(extent) - axis_at - 1))

    loudness = one(*pieces[0])
    for cut in pieces[1:]:
        loudness = loudness * one(*cut)
    return loudness


def ranked_wide(rng, shape, count, slope):
    loads = [min(1 << octave, count + 1 - (1 << octave)) * (1 << 20) // math.isqrt((1 << octave) ** slope) + 1 for octave in range((count + 1).bit_length()) if 1 << octave <= count]
    width = 1 + sum(loads) // (1 << 30)
    grid = np.cumsum(np.array([max(1, weight // width) for weight in loads]))
    pick = jax.random.randint(jax.random.fold_in(rng, 1), shape, 0, int(grid[len(loads) - 1]))
    start = jnp.left_shift(1, jnp.searchsorted(jnp.asarray(grid, jnp.int32), pick, side="right").astype(jnp.int32))
    grade = start - 1 + jax.random.randint(jax.random.fold_in(rng, 4), shape, 0, 1 << 30) % jnp.minimum(start, count + 1 - start)
    return jax.random.permutation(jax.random.fold_in(rng, 2), count)[grade].astype(jnp.int32)


def length_profile(amount, total, reach, skew):
    loads = [(1 << 20) // math.isqrt(rank ** skew) + 1 for rank in range(2, amount + 1)]
    surplus, holding = total - reach - (amount - 1), [1] * (amount - 1)
    while surplus > 0:
        candidates = [i for i in range(amount - 1) if holding[i] < reach]
        whole, budget = sum([loads[i] for i in candidates]), surplus
        for i in candidates:
            extra = min(reach - holding[i], max(1, budget * loads[i] // whole), surplus)
            holding[i] = holding[i] + extra
            surplus = surplus - extra
    return np.array([reach] + holding)


def uneven_parts(own_key, amount, total, bound, skew):
    if amount == 2:
        one = jax.random.randint(own_key, (), max(1, total - bound), min(bound, total - 1) + 1)
        return jnp.stack([one, total - one])
    lengths = jnp.asarray(length_profile(amount, total, bound, skew), jnp.int32)
    couples = (amount - 1) // 2
    giver, receiver = lengths[1:1 + 2 * couples:2], lengths[2:2 + 2 * couples:2]
    margin = jnp.minimum(giver - 1, bound - receiver)
    shifted = jax.random.randint(jax.random.fold_in(own_key, 1), (couples,), 0, 1 << 20) % (margin + 1)
    lengths = lengths.at[1:1 + 2 * couples:2].set(giver - shifted).at[2:2 + 2 * couples:2].set(receiver + shifted)
    return lengths[jax.random.permutation(jax.random.fold_in(own_key, 2), amount)]


def normal_values(key, shape, scale, limit, cuts=(), kind=jnp.bfloat16):
    values = scale * jax.random.normal(key, shape, jnp.float32)
    if cuts:
        values = values * steps_of(key, shape, cuts, -0.22, 0.18)
    return jnp.clip(values, -limit, limit).astype(kind)


def setup_inputs(seed: int = 0) -> dict:
    seeds = jax.random.split(jax.random.key(seed), 8)
    hidden = normal_values(seeds[0], (TOKENS, D), 1.0, 6.0, ((0, 8), (1, 32)))
    norm_gain = jnp.clip(jax.random.uniform(seeds[1], (D,), jnp.float32, -0.5, 0.5), -0.5, 0.5)
    weight = draw_weight(jax.random.fold_in(seeds[7], 71), 0)
    targets = touch_ends(ranked_wide(seeds[3], (N_DP, TOK_GRP), V, 2), jax.random.fold_in(seeds[3], 3), 0, V - 1).astype(jnp.int32)
    segment_ids = jax.vmap(lambda own: jnp.searchsorted(jnp.cumsum(uneven_parts(own, SEGS, TOK_GRP, TOK_GRP // 4, 0)), jnp.arange(TOK_GRP), side="right"))(jax.random.split(seeds[4], N_DP)).reshape((N_DP, TOK_GRP)).astype(jnp.int32)
    pairing = jax.vmap(lambda own: jax.random.permutation(own, SEGS))(jax.random.split(seeds[5], N_DP)).reshape((N_DP, SEGS)).astype(jnp.int32)
    ref_logp = jnp.clip(jax.random.uniform(seeds[6], (N_DP, SEGS), jnp.float32, -30.0, -20.0), -30.0, -20.0)
    return {"hidden": hidden, "norm_gain": norm_gain, "weight": weight, "targets": targets, "segment_ids": segment_ids, "pairing": pairing, "ref_logp": ref_logp}


SOFTCAP = 30.0
DPO_BETA = 0.5
LOSS_SCALE = 65536.0
EPSILON = 1e-06

def dpo_terms(token_logp, segment_ids, pairing, ref_logp):
    num_groups, group_tokens = segment_ids.shape
    seg_count = pairing.shape[1]
    pair_count = seg_count // 2
    logp_rows = token_logp.reshape(num_groups, group_tokens)
    seg_range = jnp.arange(seg_count, dtype=jnp.int32)
    member = (segment_ids[:, :, None] == seg_range[None, None, :]).astype(jnp.float32)
    counts = lax.optimization_barrier(jnp.sum(member, axis=1))
    seg_mean = lax.optimization_barrier(jnp.sum(member * logp_rows[:, :, None], axis=1)) / counts
    adjusted = seg_mean - ref_logp
    chosen_hot = (pairing[:, 0::2, None] == seg_range[None, None, :]).astype(jnp.float32)
    rejected_hot = (pairing[:, 1::2, None] == seg_range[None, None, :]).astype(jnp.float32)
    chosen = lax.optimization_barrier(jnp.sum(chosen_hot * adjusted[:, None, :], axis=2))
    rejected = lax.optimization_barrier(jnp.sum(rejected_hot * adjusted[:, None, :], axis=2))
    margins = DPO_BETA * (chosen - rejected)
    dpo_loss = jnp.mean(jax.nn.softplus(-margins))
    margin_pull = -jax.nn.sigmoid(-margins) * (LOSS_SCALE / (num_groups * pair_count))
    seg_pull = DPO_BETA * lax.optimization_barrier(jnp.sum((chosen_hot - rejected_hot) * margin_pull[:, :, None], axis=1)) / counts
    token_weight = lax.optimization_barrier(jnp.sum(member * seg_pull[:, None, :], axis=2)).reshape(-1)
    return (margins, dpo_loss, token_weight)

def reference(hidden, norm_gain, weight, targets, segment_ids, pairing, ref_logp):
    hidden32 = hidden.astype(jnp.float32)
    inv_rms = lax.rsqrt(lax.optimization_barrier(jnp.mean(hidden32 * hidden32, axis=1)) + EPSILON)
    gain_scale = 1.0 + norm_gain
    normed = (hidden32 * inv_rms[:, None] * gain_scale[None, :]).astype(jnp.bfloat16)
    weight_blocks = weight.reshape(-1, V_DEV, D)
    block_ids = jnp.arange(weight_blocks.shape[0], dtype=jnp.int32)
    flat_targets = targets.reshape(-1).astype(jnp.int32)
    tokens_all = flat_targets.shape[0]

    def block_logits(block_index, block_rows):
        raw_logits = lax.dot_general(block_rows, normed, (((1,), (1,)), ((), ())), preferred_element_type=jnp.float32)
        capped = SOFTCAP * jnp.tanh(raw_logits / SOFTCAP)
        vocab_ids = block_index * V_DEV + lax.broadcasted_iota(jnp.int32, (V_DEV, 1), 0)
        target_hot = vocab_ids == flat_targets[None, :]
        return (capped, target_hot)

    def first_pass(running, block_pair):
        capped, target_hot = block_logits(block_pair[0], block_pair[1])
        exp_part = lax.optimization_barrier(jnp.sum(jnp.exp(capped), axis=0))
        pick_part = lax.optimization_barrier(jnp.sum(jnp.where(target_hot, capped, 0.0), axis=0))
        return ((running[0] + exp_part, running[1] + pick_part), None)
    zeros_tok = jnp.zeros((tokens_all,), jnp.float32)
    (exp_total, picked), _ = lax.scan(first_pass, (zeros_tok, zeros_tok), (block_ids, weight_blocks))
    token_logp = picked - jnp.log(exp_total)
    margins, dpo_loss, token_weight = dpo_terms(token_logp, segment_ids, pairing, ref_logp)

    def second_pass(running, block_pair):
        capped, target_hot = block_logits(block_pair[0], block_pair[1])
        token_prob = jnp.exp(capped) / exp_total[None, :]
        cap_slope = 1.0 - capped / SOFTCAP * (capped / SOFTCAP)
        dlogit = (token_weight[None, :] * (target_hot.astype(jnp.float32) - token_prob) * cap_slope).astype(jnp.bfloat16)
        grad_part = lax.dot_general(dlogit, block_pair[1], (((0,), (0,)), ((), ())), preferred_element_type=jnp.float32)
        return (running + grad_part, None)
    grad_normed, _ = lax.scan(second_pass, jnp.zeros((tokens_all, D), jnp.float32), (block_ids, weight_blocks))
    row_dot = lax.optimization_barrier(jnp.sum(grad_normed * gain_scale[None, :] * hidden32, axis=1))
    hidden_grad = gain_scale[None, :] * inv_rms[:, None] * grad_normed - hidden32 * (row_dot * inv_rms * inv_rms * inv_rms / D)[:, None]
    return (hidden_grad, margins, dpo_loss)
```

```python
import jax
import jax.numpy as jnp
from jax import lax
from jax.experimental import pallas as pl
from jax.experimental.pallas import tpu as pltpu
from jax.sharding import PartitionSpec as P

SOFTCAP = 30.0
DPO_BETA = 0.5
LOSS_SCALE = 65536.0
EPSILON = 1e-06
MESH = pl.DeviceIdType.MESH

NX, NY, NZ = 4, 4, 8
D = 4608
BLK = 144
TOK = 512
LANES = 128
VOC = 1000
VPAD = 1024
GROUPS = 8
PAIRS = 4

F32 = jnp.float32
BF16 = jnp.bfloat16

SIZE = {"x": NX, "y": NY, "z": NZ}
AG_ORDER = (("z", "x", "y"), ("z", "y", "x"), ("x", "y", "z"))
RS_ORDER = (("y", "x", "z"), ("x", "y", "z"), ("z", "x", "y"))
PART_ROWS = (32, 32, 16)
PART_AT = (0, 32, 64)


def kernel(
    hidden_ref, gain_ref, w_hbm, tgt_ref, seg_ref, pair_ref, ref_ref,
    out_ref, mar_ref, loss_ref,
    w, wt, wtp, g, n, acc, ebuf, dl, dlp, gainb, hbuf, invs,
    s0, s1, s2, r01, r11, r21, t01, t11, t21, r02, r12, r22, t02, t12, t22, r03, r13, r23,
    fbuf, arz, arx, ary, arc, brz, brx, bry, brc, tbuf, mbuf,
    w_sem, core_send, core_recv, ag_send, ag_recv, fw_send, fw_recv, wt_send, wt_recv, dl_send, dl_recv,
    ar_send, ar_recv, br_send, br_recv, rs_send, rs_recv, fin_send, fin_recv,
):
    sec = lax.axis_index("section")
    grp = lax.axis_index("dp")
    me = {"x": sec // NZ, "z": sec % NZ, "y": grp // 2}
    core = grp % 2
    other = 1 - core

    def device(axis, k):
        at = dict(me)
        at[axis] = lax.rem(me[axis] + k, SIZE[axis])
        return (at["x"] * NZ + at["z"], at["y"] * 2 + core)

    partner = (sec, me["y"] * 2 + other)

    def back(axis, k):
        return lax.rem(me[axis] + (SIZE[axis] - k), SIZE[axis])

    def remote(src, dst, ssem, rsem, dev):
        return pltpu.make_async_remote_copy(
            src_ref=src, dst_ref=dst, send_sem=ssem, recv_sem=rsem, device_id=dev, device_id_type=MESH
        )

    w_copies = [
        pltpu.make_async_copy(
            w_hbm.at[:, pl.ds(x * NZ * BLK, NZ * BLK)], w.at[:, pl.ds(x * NZ * BLK, NZ * BLK)], w_sem.at[x]
        )
        for x in range(NX)
    ]
    for copy in w_copies:
        copy.start()

    barrier = pltpu.get_barrier_semaphore()
    pl.semaphore_signal(barrier, inc=1, device_id=partner, device_id_type=MESH)
    for axis in "xyz":
        for k in range(1, SIZE[axis]):
            pl.semaphore_signal(barrier, inc=1, device_id=device(axis, k), device_id_type=MESH)
    pl.semaphore_wait(barrier, 1 + NX + NY + NZ - 3)

    swap = remote(hidden_ref, hbuf.at[core], core_send, core_recv, partner)
    swap.start()
    hbuf[core] = hidden_ref[...]
    swap.wait()
    both = jnp.concatenate([hbuf[0], hbuf[1]], axis=0).astype(F32)
    both = jnp.concatenate([both, jnp.zeros((LANES, 2 * LANES - BLK), F32)], axis=1)
    own_block = jnp.transpose(both)[:BLK]
    own_block = own_block.astype(BF16)
    own_at = pl.multiple_of(80 * core, 16)
    g[me["y"], me["x"], me["z"], pl.ds(own_at, 64), :] = jnp.where(core == 0, own_block[0:64], own_block[80:144])
    g[me["y"], me["x"], me["z"], 64:80, :] = own_block[64:80]

    part_at = (80 * core, 80 * core + 32, 64)

    def g_slice(part, at):
        row = part_at[part]
        if part < 2:
            row = pl.multiple_of(row, 16)
        idx = [pl.ds(0, SIZE[a]) if at[a] is None else at[a] for a in ("y", "x", "z")]
        return g.at[idx[0], idx[1], idx[2], pl.ds(row, PART_ROWS[part]), :]

    def ag_stage(part, stage):
        axis = AG_ORDER[part][stage]
        at = dict(me)
        for done in AG_ORDER[part][:stage]:
            at[done] = None
        copies = []
        for k in range(1, SIZE[axis]):
            piece = g_slice(part, at)
            copies.append(
                remote(piece, piece, ag_send.at[part, stage, k], ag_recv.at[part, stage, k], device(axis, k))
            )
        return copies

    def forward(part, k):
        axis = AG_ORDER[part][2]
        at = {a: None for a in "xyz"}
        at[axis] = back(axis, k)
        piece = g_slice(part, at)
        return remote(piece, piece, fw_send.at[part, k], fw_recv.at[part, k], partner)

    def transpose_weight(x):
        w_copies[x].wait()
        for i in range(NZ * BLK // LANES):
            cols = w[:, pl.ds(x * NZ * BLK + i * LANES, LANES)].astype(F32)
            cols = jnp.concatenate([cols, jnp.zeros((VPAD - VOC, LANES), F32)], axis=0)
            flipped = jnp.transpose(cols).astype(BF16)
            row = i * LANES
            while row < (i + 1) * LANES:
                z, off = row // BLK, row % BLK
                count = min(BLK - off, (i + 1) * LANES - row)
                wt[x, z, off:off + count, :] = flipped[row - i * LANES:row - i * LANES + count]
                row += count

    def gain_rows(i, carry):
        row = 1.0 + gain_ref[pl.ds(i, 1), :]
        gainb[pl.ds(pl.multiple_of(i * LANES, LANES), LANES), :] = jnp.transpose(
            jnp.broadcast_to(row, (LANES, LANES))
        )
        return carry

    copies = [[ag_stage(p, s) for s in range(3)] for p in range(3)]
    for p in range(3):
        for c in copies[p][0]:
            c.start()
    transpose_weight(0)
    for s in range(1, 3):
        for p in range(3):
            for c in copies[p][s - 1]:
                c.wait()
            for c in copies[p][s]:
                c.start()
        if s == 1:
            transpose_weight(1)
    forwards = []
    for p in range(2):
        f = forward(p, 0)
        f.start()
        forwards.append(f)
    transpose_weight(2)
    for k in (0, 2, 1):
        for p in range(2):
            copies[p][2][k].wait()
            f = forward(p, k + 1)
            f.start()
            forwards.append(f)
    transpose_weight(3)
    lax.fori_loop(0, D // LANES, gain_rows, 0)
    for c in copies[2][2]:
        c.wait()
    for f in forwards:
        f.wait()

    far = pl.multiple_of(80 * other, 16)
    wt_copies = [
        remote(wt.at[:, :, pl.ds(far, 64), :], wtp.at[:, :, pl.ds(0, 64), :], wt_send.at[0], wt_recv.at[0], partner),
        remote(wt.at[:, :, pl.ds(64, 16), :], wtp.at[:, :, pl.ds(64, 16), :], wt_send.at[1], wt_recv.at[1], partner),
    ]
    for c in wt_copies:
        c.start()

    def squares(i, sums):
        x, z = i // NZ, i % NZ
        res = []
        for y in range(NY):
            h = g[y, x, z].astype(F32)
            res.append(sums[y] + jnp.sum((h * h).reshape(BLK // 8, 8, LANES), axis=0))
        return tuple(res)

    sums = lax.fori_loop(0, NX * NZ, squares, tuple(jnp.zeros((8, LANES), F32) for _ in range(NY)))
    mean_sq = jnp.concatenate([jnp.sum(v, axis=0, keepdims=True) for v in sums], axis=0) / D
    inv = lax.rsqrt(mean_sq + EPSILON)
    invs[0:NY, :] = inv

    def normalize(i, carry):
        x, z = i // NZ, i % NZ
        rows = pl.ds(pl.multiple_of(i * BLK, BLK), BLK)
        gain = gainb[rows, :]
        for y in range(NY):
            h = g[y, x, z].astype(F32)
            n[rows, y * LANES:(y + 1) * LANES] = (h * inv[y:y + 1] * gain).astype(BF16)
        return carry

    lax.fori_loop(0, NX * NZ, normalize, 0)

    depth = 256
    acc[0:VOC, :] = jnp.dot(w[:, 0:depth], n[0:depth, :], preferred_element_type=F32)

    def logits(i, carry):
        at = pl.ds(pl.multiple_of(i * depth, depth), depth)
        acc[0:VOC, :] += jnp.dot(w[:, at], n[at, :], preferred_element_type=F32)
        return carry

    lax.fori_loop(1, D // depth, logits, 0)

    tile = 128
    vocab_start = (sec * 2 * NY + grp) * VOC
    targets = tgt_ref[...]

    def row_ids(i):
        return i * tile + lax.broadcasted_iota(jnp.int32, (tile, TOK), 0)

    def fold(v):
        return jnp.sum(v.reshape(tile // 8, 8, TOK), axis=0)

    def softmax_tile(i, carry):
        tot, pick = carry
        at = pl.ds(pl.multiple_of(i * tile, tile), tile)
        ids = row_ids(i)
        valid = ids < VOC
        capped = SOFTCAP * jnp.tanh(acc[at, :] * (1.0 / SOFTCAP))
        e = jnp.where(valid, jnp.exp(capped), 0.0)
        ebuf[at, :] = e
        hot = jnp.logical_and(ids + vocab_start == targets, valid)
        return (tot + fold(e), pick + fold(jnp.where(hot, capped, 0.0)))

    zero = jnp.zeros((8, TOK), F32)
    tot, pick = lax.fori_loop(0, VPAD // tile, softmax_tile, (zero, zero))

    def to_rows(v):
        v = jnp.sum(v, axis=0, keepdims=True)
        return [v[:, y * LANES:(y + 1) * LANES] for y in range(NY)]

    def reduce_copies(buf, axis, ssem, rsem, stage):
        if axis == "c":
            piece = buf.at[core]
            return [remote(piece, piece, ssem.at[stage, 0], rsem.at[stage, 0], partner)]
        piece = buf.at[me[axis]]
        return [
            remote(piece, piece, ssem.at[stage, k], rsem.at[stage, k], device(axis, k)) for k in range(1, SIZE[axis])
        ]

    def reduce_start(value, buf, axis, ssem, rsem, stage):
        buf[core if axis == "c" else me[axis]] = value
        cs = reduce_copies(buf, axis, ssem, rsem, stage)
        for c in cs:
            c.start()
        return cs

    def reduce_end(cs, buf):
        for c in cs:
            c.wait()
        return jnp.sum(buf[...], axis=0)

    value = jnp.concatenate(to_rows(tot) + to_rows(pick), axis=0)
    for stage, (axis, buf) in enumerate((("z", arz), ("x", arx), ("y", ary), ("c", arc))):
        value = reduce_end(reduce_start(value, buf, axis, ar_send, ar_recv, stage), buf)

    exp_total = value[0:NY]
    logp = value[NY:2 * NY] - jnp.log(exp_total)

    def twice(v):
        return jnp.concatenate([v[r // 2:r // 2 + 1] for r in range(GROUPS)], axis=0)

    lane = lax.broadcasted_iota(jnp.int32, (GROUPS, LANES), 1)
    group = lax.broadcasted_iota(jnp.int32, (GROUPS, LANES), 0)
    own_half = (lane // 64) == (group % 2)
    seg = jnp.where(own_half, twice(seg_ref[...]), -1)
    logp = twice(logp)
    pairing = pair_ref[...]
    ref_logp = ref_ref[...]
    members, counts, adjusted = [], [], []
    for s in range(GROUPS):
        member = (seg == s).astype(F32)
        count = jnp.sum(member, axis=1, keepdims=True)
        members.append(member)
        counts.append(count)
        adjusted.append(jnp.sum(member * logp, axis=1, keepdims=True) / count - ref_logp[:, s:s + 1])
    margins, pulls, hots = [], [], []
    loss = jnp.zeros((GROUPS, 1), F32)
    for k in range(PAIRS):
        signs = [
            (pairing[:, 2 * k:2 * k + 1] == s).astype(F32) - (pairing[:, 2 * k + 1:2 * k + 2] == s).astype(F32)
            for s in range(GROUPS)
        ]
        margin = DPO_BETA * sum(sign * a for sign, a in zip(signs, adjusted))
        loss = loss + jnp.maximum(-margin, 0.0) + jnp.log1p(jnp.exp(-jnp.abs(margin)))
        hots.append(signs)
        margins.append(margin)
        pulls.append(-jax.nn.sigmoid(-margin) * (LOSS_SCALE / (GROUPS * PAIRS)))
    weight_rows = jnp.zeros((GROUPS, LANES), F32)
    for s in range(GROUPS):
        pull = DPO_BETA * sum(hots[k][s] * pulls[k] for k in range(PAIRS)) / counts[s]
        weight_rows = weight_rows + members[s] * pull
    token_weight = jnp.concatenate(
        [weight_rows[2 * y:2 * y + 1] + weight_rows[2 * y + 1:2 * y + 2] for y in range(NY)], axis=1
    )
    inv_total = 1.0 / exp_total
    inv_total = jnp.concatenate([inv_total[y:y + 1] for y in range(NY)], axis=1)

    def grad_tile(i, row_dot):
        at = pl.ds(pl.multiple_of(i * tile, tile), tile)
        ids = row_ids(i)
        valid = ids < VOC
        raw = acc[at, :]
        th = jnp.tanh(raw * (1.0 / SOFTCAP))
        hot = (ids + vocab_start == targets).astype(F32)
        d = token_weight * (hot - ebuf[at, :] * inv_total) * (1.0 - th * th)
        d = jnp.where(valid, d, 0.0).astype(BF16)
        dl[at, :] = d
        d = d.astype(F32)
        return row_dot + fold(jnp.where(d == 0.0, 0.0, d * raw))

    row_dot = zero
    dl_copies = []
    for q in range(4):
        row_dot = lax.fori_loop(2 * q, 2 * q + 2, grad_tile, row_dot)
        at = pl.ds(q * 2 * tile, 2 * tile)
        c = remote(dl.at[at, :], dlp.at[at, :], dl_send.at[q], dl_recv.at[q], partner)
        c.start()
        dl_copies.append(c)

    br_value = jnp.concatenate(to_rows(row_dot) + [jnp.zeros((NY, LANES), F32)], axis=0)
    br_copies = reduce_start(br_value, brz, "z", br_send, br_recv, 0)

    col = lax.broadcasted_iota(jnp.int32, (GROUPS, LANES), 1)
    mbuf[...] = sum(jnp.where(col == k, margins[k], 0.0) for k in range(PAIRS))
    mar_ref[...] = mbuf[pl.ds(grp, 1), :][:, 0:PAIRS]
    loss_ref[...] = jnp.sum(loss, axis=0, keepdims=True) * (1.0 / (GROUPS * PAIRS))

    for c in wt_copies:
        c.wait()
    for c in dl_copies:
        c.wait()

    def terms(part, xs, s):
        rows = PART_ROWS[part]
        near = part_at[part] if part == 2 else pl.multiple_of(part_at[part], 16)

        def body(i, carry):
            a = wt[pl.ds(i * xs, xs), :, pl.ds(near, rows), :].reshape(xs * NZ * rows, VPAD)
            b = wtp[pl.ds(i * xs, xs), :, pl.ds(PART_AT[part], rows), :].reshape(xs * NZ * rows, VPAD)
            t = jnp.dot(a, dl[...], preferred_element_type=F32)
            t = t + jnp.dot(b, dlp[...], preferred_element_type=F32)
            t = t.astype(BF16)
            for y in range(NY):
                s[y, pl.ds(i * xs, xs)] = t[:, y * LANES:(y + 1) * LANES].reshape(xs, NZ, rows, LANES)
            return carry

        lax.fori_loop(0, NX // xs, body, 0)

    def scatter(part, stage, src, dst):
        axis = RS_ORDER[part][stage]
        cs = []
        for k in range(1, SIZE[axis]):
            to = lax.rem(me[axis] + k, SIZE[axis])
            cs.append(
                remote(src(to), dst.at[me[axis]], rs_send.at[part, stage, k], rs_recv.at[part, stage, k], device(axis, k))
            )
        for c in cs:
            c.start()
        return cs

    def total(part, stage, cs, own, dst):
        axis = RS_ORDER[part][stage]
        for c in cs:
            c.wait()
        return [own] + [dst.at[back(axis, k)] for k in range(1, SIZE[axis])]

    def add_up(refs, lead, out):
        def body(i, carry):
            v = refs[0][i].astype(F32)
            for r in refs[1:]:
                v = v + r[i].astype(F32)
            out[i] = v.astype(BF16)
            return carry

        lax.fori_loop(0, lead, body, 0)

    terms(2, 4, s2)
    c2 = scatter(2, 0, lambda to: s2.at[:, :, to], r21)
    terms(0, 2, s0)
    c0 = scatter(0, 0, lambda to: s0.at[to], r01)
    terms(1, 2, s1)
    c1 = scatter(1, 0, lambda to: s1.at[:, to], r11)

    br_value = reduce_end(br_copies, brz)
    br_copies = reduce_start(br_value, brx, "x", br_send, br_recv, 1)

    add_up(total(1, 0, c1, s1.at[:, me["x"]], r11), NY, t11)
    c1 = scatter(1, 1, lambda to: t11.at[to], r12)
    br_value = reduce_end(br_copies, brx)
    br_copies = reduce_start(br_value, bry, "y", br_send, br_recv, 2)
    add_up(total(0, 0, c0, s0.at[me["y"]], r01), NX, t01)
    c0 = scatter(0, 1, lambda to: t01.at[to], r02)
    add_up(total(2, 0, c2, s2.at[:, :, me["z"]], r21), NY, t21)
    c2 = scatter(2, 1, lambda to: t21.at[:, to], r22)
    br_value = reduce_end(br_copies, bry)
    br_copies = reduce_start(br_value, brc, "c", br_send, br_recv, 3)

    add_up(total(1, 1, c1, t11.at[me["y"]], r12), NZ, t12)
    c1 = scatter(1, 2, lambda to: t12.at[to], r13)
    add_up(total(0, 1, c0, t01.at[me["x"]], r02), NZ, t02)
    c0 = scatter(0, 2, lambda to: t02.at[to], r03)
    add_up(total(2, 1, c2, t21.at[:, me["x"]], r22), NY, t22)
    c2 = scatter(2, 2, lambda to: t22.at[to], r23)
    row_dot = reduce_end(br_copies, brc)
    tbuf[0:8, :] = row_dot

    def last(refs):
        v = refs[0][...].astype(F32)
        for r in refs[1:]:
            v = v + r[...].astype(F32)
        return v

    fbuf[pl.ds(64, 16), :] = last(total(2, 2, c2, t22.at[me["y"]], r23))
    fbuf[pl.ds(pl.multiple_of(80 * core, 16), 32), :] = last(total(0, 2, c0, t02.at[me["z"]], r03))
    fbuf[pl.ds(pl.multiple_of(80 * core + 32, 16), 32), :] = last(total(1, 2, c1, t12.at[me["z"]], r13))
    mine = fbuf.at[pl.ds(pl.multiple_of(80 * core, 16), 64), :]
    swap = remote(mine, mine, fin_send, fin_recv, partner)
    swap.start()
    swap.wait()

    own_inv = invs[pl.ds(me["y"], 1), :]
    own_dot = tbuf[pl.ds(me["y"], 1), :]
    own_gain = gainb[pl.ds(pl.multiple_of(sec * BLK, BLK), BLK), :]
    own_hidden = g[me["y"], me["x"], me["z"]].astype(F32)
    result = own_gain * own_inv * fbuf[...] - own_hidden * (own_dot * own_inv * own_inv * (1.0 / D))
    result = jnp.concatenate([result, jnp.zeros((2 * LANES - BLK, LANES), F32)], axis=0)
    flipped = jnp.transpose(result)
    out_ref[...] = jnp.where(core == 0, flipped[0:64, 0:BLK], flipped[64:128, 0:BLK])


def per_device(hidden, norm_gain, weight, targets, segment_ids, pairing, ref_logp):
    vmem = pl.BlockSpec(memory_space=pltpu.VMEM)
    dma = pltpu.SemaphoreType.DMA
    V = pltpu.VMEM
    grad, margins, loss = pl.pallas_call(
        kernel,
        out_shape=(
            jax.ShapeDtypeStruct((64, BLK), F32),
            jax.ShapeDtypeStruct((1, PAIRS), F32),
            jax.ShapeDtypeStruct((1, 1), F32),
        ),
        in_specs=[vmem, vmem, pl.BlockSpec(memory_space=pl.ANY), vmem, vmem, vmem, vmem],
        out_specs=(vmem, vmem, vmem),
        scratch_shapes=[
            V((VOC, D), BF16),
            V((NX, NZ, BLK, VPAD), BF16),
            V((NX, NZ, 80, VPAD), BF16),
            V((NY, NX, NZ, BLK, LANES), BF16),
            V((D, TOK), BF16),
            V((VPAD, TOK), F32),
            V((VPAD, TOK), F32),
            V((VPAD, TOK), BF16),
            V((VPAD, TOK), BF16),
            V((D, LANES), F32),
            V((2, 64, BLK), BF16),
            V((8, LANES), F32),
            V((NY, NX, NZ, 32, LANES), BF16),
            V((NY, NX, NZ, 32, LANES), BF16),
            V((NY, NX, NZ, 16, LANES), BF16),
            V((NY, NX, NZ, 32, LANES), BF16),
            V((NX, NY, NZ, 32, LANES), BF16),
            V((NZ, NY, NX, 16, LANES), BF16),
            V((NX, NZ, 32, LANES), BF16),
            V((NY, NZ, 32, LANES), BF16),
            V((NY, NX, 16, LANES), BF16),
            V((NX, NZ, 32, LANES), BF16),
            V((NY, NZ, 32, LANES), BF16),
            V((NX, NY, 16, LANES), BF16),
            V((NZ, 32, LANES), BF16),
            V((NZ, 32, LANES), BF16),
            V((NY, 16, LANES), BF16),
            V((NZ, 32, LANES), BF16),
            V((NZ, 32, LANES), BF16),
            V((NY, 16, LANES), BF16),
            V((BLK, LANES), F32),
            V((NZ, 8, LANES), F32),
            V((NX, 8, LANES), F32),
            V((NY, 8, LANES), F32),
            V((2, 8, LANES), F32),
            V((NZ, 8, LANES), F32),
            V((NX, 8, LANES), F32),
            V((NY, 8, LANES), F32),
            V((2, 8, LANES), F32),
            V((8, LANES), F32),
            V((8, LANES), F32),
            dma((NX,)),
            dma, dma,
            dma((3, 3, NZ)), dma((3, 3, NZ)),
            dma((2, 4)), dma((2, 4)),
            dma((2,)), dma((2,)),
            dma((4,)), dma((4,)),
            dma((4, NZ)), dma((4, NZ)),
            dma((4, NZ)), dma((4, NZ)),
            dma((3, 3, NZ)), dma((3, 3, NZ)),
            dma, dma,
        ],
        compiler_params=pltpu.CompilerParams(
            collective_id=0, has_side_effects=True, vmem_limit_bytes=60 * 2**20
        ),
        name="dpo_output_layer",
    )(
        hidden,
        norm_gain.reshape(D // LANES, LANES),
        weight,
        targets.reshape(1, TOK),
        segment_ids.reshape(NY, LANES),
        pairing,
        ref_logp,
    )
    return (grad, margins, loss.reshape(()))


def solution(mesh):
    in_specs = (P("dp", "section"), P(), P(("section", "dp"), None), P(), P(), P(), P())
    out_specs = (P("dp", "section"), P("dp", None), P())
    return jax.shard_map(
        per_device, mesh=mesh, in_specs=in_specs, out_specs=out_specs, check_vma=False
    )
```

```python
import jax
import jax.numpy as jnp
from jax import lax
from jax.experimental import pallas as pl
from jax.experimental.pallas import tpu as pltpu
from jax.sharding import PartitionSpec as P

SOFTCAP = 30.0
DPO_BETA = 0.5
LOSS_SCALE = 65536.0
EPSILON = 1e-06
MESH = pl.DeviceIdType.MESH

NX, NY, NZ = 4, 4, 8
D = 4608
BLK = 144
TOK = 512
LANES = 128
VOC = 1000
VPAD = 1024
V_ALL = 256000
GROUPS = 8
PAIRS = 4

F32 = jnp.float32
BF16 = jnp.bfloat16

SIZE = {"x": NX, "y": NY, "z": NZ}
AG_ORDER = (("z", "x", "y"), ("z", "y", "x"), ("y", "x", "z"))
OWN = 64
MID = 16
RS_ORDER = (("y", "x", "z"), ("x", "y", "z"), ("z", "x", "y"))
PART_ROWS = (32, 32, 16)
PART_AT = (0, 32, 64)


def kernel(
    hid_hbm, gain_hbm, w_hbm, tgt_hbm, seg_hbm, pair_hbm, ref_hbm,
    out_ref, mar_ref, loss_ref,
    gain_ref, tgt_ref, seg_ref, pair_ref, ref_ref,
    w, wt, wtp, g, n, acc, hot, hotp, dl, dlp, gainb, hbuf, invs,
    u0, u1, u2, a0, a1, a2,
    s0, s1, s2, r01, r11, r21, t01, t11, t21, r02, r12, r22, t02, t12, t22, r03, r13, r23,
    fbuf, arz, arx, ary, arc, sqz, sqx, sqy, coef, dotb, mbuf,
    in_sem, w_sem, core_send, core_recv, ag1_send, ag1_recv, ag2_send, ag2_recv, ag3_send, ag3_recv, fw_send, fw_recv,
    wt_send, wt_recv, dl_send, dl_recv, ar_send, ar_recv, sq_send, sq_recv,
    rs1_send, rs1_recv, rs2_send, rs2_recv, rs3_send, rs3_recv, fin_send, fin_recv,
):
    sec = lax.axis_index("section")
    grp = lax.axis_index("dp")
    me = {"x": sec // NZ, "z": sec % NZ, "y": grp // 2}
    core = grp % 2
    other = 1 - core

    def device(axis, k):
        at = dict(me)
        at[axis] = ahead(axis, k)
        return (at["x"] * NZ + at["z"], at["y"] * 2 + core)

    partner = (sec, me["y"] * 2 + other)

    def ahead(axis, k):
        return lax.rem(me[axis] + k, SIZE[axis])

    def back(axis, k):
        return lax.rem(me[axis] + (SIZE[axis] - k), SIZE[axis])

    def remote(src, dst, ssem, rsem, dev):
        return pltpu.make_async_remote_copy(
            src_ref=src, dst_ref=dst, send_sem=ssem, recv_sem=rsem, device_id=dev, device_id_type=MESH
        )

    def start(copies):
        for c in copies:
            c.start()
        return copies

    def wait(copies):
        for c in copies:
            c.wait()

    cut = NZ * BLK
    small = ((hid_hbm, hbuf.at[core]), (gain_hbm, gain_ref), (tgt_hbm, tgt_ref), (seg_hbm, seg_ref),
             (pair_hbm, pair_ref), (ref_hbm, ref_ref))
    in_copies = start([pltpu.make_async_copy(src, dst, in_sem.at[i]) for i, (src, dst) in enumerate(small)])
    w_copies = start([
        pltpu.make_async_copy(w_hbm.at[:, pl.ds(x * cut, cut)], w.at[:, pl.ds(x * cut, cut)], w_sem.at[x])
        for x in range(NX)
    ])

    barrier = pltpu.get_barrier_semaphore()
    pl.semaphore_signal(barrier, inc=1, device_id=partner, device_id_type=MESH)
    for axis in "xyz":
        for k in range(1, SIZE[axis]):
            pl.semaphore_signal(barrier, inc=1, device_id=device(axis, k), device_id_type=MESH)
    pl.semaphore_wait(barrier, 1 + NX + NY + NZ - 3)

    in_copies[0].wait()
    swap = remote(hbuf.at[core], hbuf.at[core], core_send, core_recv, partner)
    swap.start()
    wait(in_copies[1:])
    swap.wait()
    both = jnp.concatenate([hbuf[0], hbuf[1]], axis=0).astype(F32)
    both = jnp.concatenate([both, jnp.zeros((LANES, 2 * LANES - BLK), F32)], axis=1)
    own_block = jnp.transpose(both)[:BLK]
    own_bits = own_block.astype(BF16)
    own_at = pl.multiple_of(80 * core, 16)
    g[me["y"], me["x"], me["z"], pl.ds(own_at, 64), :] = jnp.where(core == 0, own_bits[0:64], own_bits[80:144])
    g[me["y"], me["x"], me["z"], 64:80, :] = own_bits[64:80]

    part_at = (own_at, pl.multiple_of(80 * core + 32, 16), OWN)

    def g_slice(at, row, rows):
        idx = [at[a] if a in at else pl.ds(0, SIZE[a]) for a in ("y", "x", "z")]
        return g.at[idx[0], idx[1], idx[2], pl.ds(row, rows), :]

    def ag_first(i, axis, row, rows):
        piece = g_slice(me, row, rows)
        return [
            remote(piece, piece, ag1_send.at[i, k], ag1_recv.at[i, k], device(axis, k)) for k in range(1, SIZE[axis])
        ]

    def ag_second(part):
        first, axis, _ = AG_ORDER[part]
        piece = g_slice({a: me[a] for a in me if a != first}, part_at[part], PART_ROWS[part])
        return [
            remote(piece, piece, ag2_send.at[part, k], ag2_recv.at[part, k], device(axis, k)) for k in range(1, 4)
        ]

    def ag_last(part, j):
        _, second, third = AG_ORDER[part]
        piece = g_slice({second: back(second, j), third: me[third]}, part_at[part], PART_ROWS[part])
        return [
            remote(piece, piece, ag3_send.at[part, j, k], ag3_recv.at[part, j, k], device(third, k))
            for k in range(1, SIZE[third])
        ]

    forwards = {}

    def forward(part, j, k):
        _, second, third = AG_ORDER[part]
        piece = g_slice({second: back(second, j), third: back(third, k)}, part_at[part], PART_ROWS[part])
        c = remote(piece, piece, fw_send.at[part, j, k], fw_recv.at[part, j, k], partner)
        c.start()
        forwards[part, j, k] = c

    def sum_copies(buf, axis, ssem, rsem, stage):
        if axis == "c":
            piece = buf.at[core]
            return [remote(piece, piece, ssem.at[stage, 0], rsem.at[stage, 0], partner)]
        piece = buf.at[me[axis]]
        return [
            remote(piece, piece, ssem.at[stage, k], rsem.at[stage, k], device(axis, k)) for k in range(1, SIZE[axis])
        ]

    def sum_start(value, buf, axis, ssem, rsem, stage):
        buf[core if axis == "c" else me[axis]] = value
        return start(sum_copies(buf, axis, ssem, rsem, stage))

    def sum_end(copies, buf):
        wait(copies)
        return jnp.sum(buf[...], axis=0)

    stage1 = start(ag_first(0, "z", own_at, OWN))
    mid1 = start(ag_first(1, "y", OWN, MID))
    squares = jnp.sum((own_block * own_block).reshape(BLK // 8, 8, LANES), axis=0)
    sq = sum_start(squares, sqz, "z", sq_send, sq_recv, 0)

    def transpose_weight(x):
        w_copies[x].wait()
        for i in range(cut // LANES):
            cols = w[:, pl.ds(x * cut + i * LANES, LANES)].astype(F32)
            cols = jnp.concatenate([cols, jnp.zeros((VPAD - VOC, LANES), F32)], axis=0)
            flipped = jnp.transpose(cols).astype(BF16)
            row = i * LANES
            while row < (i + 1) * LANES:
                z, off = row // BLK, row % BLK
                count = min(BLK - off, (i + 1) * LANES - row)
                wt[x, z, off:off + count, :] = flipped[row - i * LANES:row - i * LANES + count]
                row += count

    def gain_rows(i, carry):
        for q in range(4):
            row = 1.0 + gain_ref[pl.ds(4 * i + q, 1), :]
            gainb[pl.ds(pl.multiple_of((4 * i + q) * LANES, LANES), LANES), :] = jnp.transpose(
                jnp.broadcast_to(row, (LANES, LANES))
            )
        return carry

    stage2, stage3 = {}, {}

    def first_done(p):
        stage2[p] = start(ag_second(p))
        stage3[p, 0] = start(ag_last(p, 0))
        if p < 2:
            forward(p, 0, 0)

    transpose_weight(0)
    transpose_weight(1)
    wait(mid1)
    first_done(2)
    transpose_weight(2)
    transpose_weight(3)
    wait(stage1)
    first_done(0)
    first_done(1)
    sq = sum_start(sum_end(sq, sqz), sqx, "x", sq_send, sq_recv, 1)

    tile = 128
    vocab_start = (sec * 2 * NY + grp) * VOC
    other_start = (sec * 2 * NY + me["y"] * 2 + other) * VOC
    half = lax.broadcasted_iota(jnp.int32, (1, LANES), 1) < 64
    tgt = jnp.concatenate([tgt_ref[...], tgt_ref[...]], axis=1)
    targets = jnp.concatenate(
        [jnp.where(half, tgt[2 * y:2 * y + 1], tgt[2 * y + 1:2 * y + 2]) for y in range(NY)], axis=1
    )

    def row_ids(i):
        return i * tile + lax.broadcasted_iota(jnp.int32, (tile, TOK), 0)

    def hot_tile(i, carry):
        at = pl.ds(pl.multiple_of(i * tile, tile), tile)
        ids = row_ids(i)
        ids = jnp.where(ids < VOC, ids, -2 * V_ALL)
        hot[at, :] = (ids + vocab_start == targets).astype(F32).astype(BF16)
        hotp[at, :] = (ids + other_start == targets).astype(F32).astype(BF16)
        return carry


    def rows_product(part, xs, mine, right, out, add):
        rows = PART_ROWS[part]
        ref, at = (wt, part_at[part]) if mine else (wtp, PART_AT[part])

        def body(i, carry):
            xat = pl.ds(i * xs, xs)
            left = ref[xat, :, pl.ds(at, rows), :].reshape(xs * NZ * rows, VPAD)
            t = jnp.dot(left, right[...], preferred_element_type=F32).reshape(xs, NZ * rows, TOK)
            if add:
                t = t + out[xat].astype(F32)
            out[xat] = t.astype(out.dtype)
            return carry

        lax.fori_loop(0, NX // xs, body, 0)

    def product(mine, right, outs, add):
        for part, xs in ((0, 2), (1, 2), (2, 4)):
            rows_product(part, xs, mine, right, outs[part], add)

    for j in (1, 3, 2):
        for p in (2, 0, 1):
            stage2[p][j - 1].wait()
            stage3[p, j] = start(ag_last(p, j))
            if p < 2:
                forward(p, j, 0)
    sq = sum_start(sum_end(sq, sqx), sqy, "y", sq_send, sq_recv, 2)
    lax.fori_loop(0, D // LANES // 4, gain_rows, 0)
    lax.fori_loop(0, VPAD // tile, hot_tile, 0)
    product(True, hot, (a0, a1, a2), False)

    wait(sq)
    mean_sq = jnp.concatenate([jnp.sum(sqy[y], axis=0, keepdims=True) for y in range(NY)], axis=0) / D
    invs[0:NY, :] = lax.rsqrt(mean_sq + EPSILON)

    def pass_on(j):
        for k in (1, 3, 2):
            stage3[0, j][k - 1].wait()
            forward(0, j, k)
        if j > 0:
            for jj in (0, 1, 3, 2):
                stage3[1, jj][j - 1].wait()
                forward(1, jj, j)

    def logits(j, first):
        wait(stage3[2, j])
        for k in range(4):
            forwards[0, j, k].wait()
            forwards[1, k, j].wait()
        xb = back("x", j)

        def normalize(z, carry):
            rows = pl.ds(pl.multiple_of(z * BLK, BLK), BLK)
            gain = gainb[pl.ds(pl.multiple_of((xb * NZ + z) * BLK, BLK), BLK), :]
            for y in range(NY):
                h = g[y, xb, z].astype(F32)
                n[rows, y * LANES:(y + 1) * LANES] = (h * invs[y:y + 1, :] * gain).astype(BF16)
            return carry

        lax.fori_loop(0, NZ, normalize, 0)
        t = jnp.dot(w[:, pl.ds(pl.multiple_of(xb * cut, LANES), cut)], n[...], preferred_element_type=F32)
        if first:
            acc[0:VOC, :] = t
        else:
            acc[0:VOC, :] += t

    pass_on(0)
    pass_on(1)
    logits(0, True)
    pass_on(3)
    logits(1, False)
    pass_on(2)
    far = pl.multiple_of(80 * other, 16)
    wt_copies = start([
        remote(wt.at[:, :, pl.ds(far, 64), :], wtp.at[:, :, pl.ds(0, 64), :], wt_send.at[0], wt_recv.at[0], partner),
        remote(wt.at[:, :, pl.ds(64, 16), :], wtp.at[:, :, pl.ds(64, 16), :], wt_send.at[1], wt_recv.at[1], partner),
    ])
    logits(3, False)
    logits(2, False)

    def fold(v):
        return jnp.sum(v.reshape(tile // 8, 8, TOK), axis=0)

    def softmax_tile(i, carry):
        tot, pick, dots = carry
        at = pl.ds(pl.multiple_of(i * tile, tile), tile)
        ids = row_ids(i)
        valid = ids < VOC
        raw = acc[at, :]
        th = jnp.tanh(raw * (1.0 / SOFTCAP))
        e = jnp.where(valid, jnp.exp(SOFTCAP * th), 0.0)
        at_target = jnp.logical_and(ids + vocab_start == targets, valid)
        term = jnp.where(jnp.logical_or(at_target, jnp.logical_not(valid)), 0.0, e * (1.0 - th * th)).astype(BF16)
        dl[at, :] = term
        term = term.astype(F32)
        return (
            tot + fold(e),
            pick + fold(jnp.where(at_target, raw, 0.0)),
            dots + fold(jnp.where(term == 0.0, 0.0, term * raw)),
        )

    zero = jnp.zeros((8, TOK), F32)
    carry = (zero, zero, zero)
    dl_copies = []
    for q in range(4):
        carry = lax.fori_loop(2 * q, 2 * q + 2, softmax_tile, carry)
        at = pl.ds(q * 2 * tile, 2 * tile)
        dl_copies += start([remote(dl.at[at, :], dlp.at[at, :], dl_send.at[q], dl_recv.at[q], partner)])

    def to_rows(v):
        v = jnp.sum(v, axis=0, keepdims=True)
        return [v[:, y * LANES:(y + 1) * LANES] for y in range(NY)]

    value = jnp.concatenate(
        to_rows(carry[0]) + to_rows(carry[1]) + to_rows(carry[2]) + [jnp.zeros((NY, LANES), F32)], axis=0
    )
    sums = sum_start(value, arz, "z", ar_send, ar_recv, 0)
    product(True, dl, (u0, u1, u2), False)
    sums = sum_start(sum_end(sums, arz), arx, "x", ar_send, ar_recv, 1)
    wait(wt_copies)
    product(False, hotp, (a0, a1, a2), True)
    sums = sum_start(sum_end(sums, arx), ary, "y", ar_send, ar_recv, 2)
    wait(dl_copies)
    product(False, dlp, (u0, u1, u2), True)
    sums = sum_start(sum_end(sums, ary), arc, "c", ar_send, ar_recv, 3)
    value = sum_end(sums, arc)

    exp_total = value[0:NY]
    target_raw = value[NY:2 * NY]
    dots = value[2 * NY:3 * NY]
    target_th = jnp.tanh(target_raw * (1.0 / SOFTCAP))
    target_capped = SOFTCAP * target_th
    logp = target_capped - jnp.log(exp_total)

    lane = lax.broadcasted_iota(jnp.int32, (GROUPS, LANES), 1)
    group = lax.broadcasted_iota(jnp.int32, (GROUPS, LANES), 0)
    own_half = (lane // 64) == (group % 2)
    seg = jnp.where(own_half, jnp.concatenate([seg_ref[...], seg_ref[...]], axis=1), -1)
    logp = jnp.concatenate([logp[r // 2:r // 2 + 1] for r in range(GROUPS)], axis=0)
    pairing = pair_ref[...]
    ref_logp = ref_ref[...]
    members, counts, adjusted = [], [], []
    for s in range(GROUPS):
        member = (seg == s).astype(F32)
        count = jnp.sum(member, axis=1, keepdims=True)
        members.append(member)
        counts.append(count)
        adjusted.append(jnp.sum(member * logp, axis=1, keepdims=True) / count - ref_logp[:, s:s + 1])
    margins, pulls, hots = [], [], []
    loss = jnp.zeros((GROUPS, 1), F32)
    for k in range(PAIRS):
        signs = [
            (pairing[:, 2 * k:2 * k + 1] == s).astype(F32) - (pairing[:, 2 * k + 1:2 * k + 2] == s).astype(F32)
            for s in range(GROUPS)
        ]
        margin = DPO_BETA * sum(sign * a for sign, a in zip(signs, adjusted))
        loss = loss + jnp.maximum(-margin, 0.0) + jnp.log1p(jnp.exp(-jnp.abs(margin)))
        hots.append(signs)
        margins.append(margin)
        pulls.append(-jax.nn.sigmoid(-margin) * (LOSS_SCALE / (GROUPS * PAIRS)))
    weight_rows = jnp.zeros((GROUPS, LANES), F32)
    for s in range(GROUPS):
        pull = DPO_BETA * sum(hots[k][s] * pulls[k] for k in range(PAIRS)) / counts[s]
        weight_rows = weight_rows + members[s] * pull
    token_weight = jnp.concatenate(
        [weight_rows[2 * y:2 * y + 1] + weight_rows[2 * y + 1:2 * y + 2] for y in range(NY)], axis=0
    )
    inv_total = 1.0 / exp_total
    at_target = token_weight * (1.0 - jnp.exp(target_capped) * inv_total) * (1.0 - target_th * target_th)
    elsewhere = -token_weight * inv_total
    coef[0:NY, :] = at_target
    coef[NY:2 * NY, :] = elsewhere
    dotb[0:NY, :] = jnp.where(at_target == 0.0, 0.0, at_target * target_raw) + elsewhere * dots

    s_bufs, r1, t1, r2 = (s0, s1, s2), (r01, r11, r21), (t01, t11, t21), (r02, r12, r22)
    t2, r3 = (t02, t12, t22), (r03, r13, r23)
    u_bufs, a_bufs = (u0, u1, u2), (a0, a1, a2)

    def blend(part, y, xb):
        rows = PART_ROWS[part]
        at = pl.ds(pl.multiple_of(y * LANES, LANES), LANES)
        v = coef[pl.ds(y, 1), :] * a_bufs[part][xb, :, at].astype(F32)
        v = v + coef[pl.ds(NY + y, 1), :] * u_bufs[part][xb, :, at]
        return v.astype(BF16).reshape(NZ, rows, LANES)

    def blend_part(part, j):
        def body(i, carry):
            if part == 0:
                s0[i, ahead("x", j)] = blend(0, i, ahead("x", j))
            elif part == 1:
                s1[i, ahead("y", j)] = blend(1, ahead("y", j), i)
            else:
                s2[ahead("x", j), :, i] = blend(2, i, ahead("x", j))
            return carry

        lax.fori_loop(0, 4, body, 0)

    def scatter1(part, j):
        first, second, _ = RS_ORDER[part]
        to2 = ahead(second, j)
        copies = []
        for k in range(1, SIZE[first]):
            to1 = ahead(first, k)
            src = s2.at[to2, to1] if part == 2 else s_bufs[part].at[to1, to2]
            copies.append(
                remote(src, r1[part].at[me[first], to2], rs1_send.at[part, j, k], rs1_recv.at[part, j, k],
                       device(first, k))
            )
        return start(copies)

    def gather1(part, j):
        first, second, _ = RS_ORDER[part]
        wait(scat1[part, j])
        to2 = ahead(second, j)
        own = s2.at[to2, me["z"]] if part == 2 else s_bufs[part].at[me[first], to2]
        return [own] + [r1[part].at[back(first, k), to2] for k in range(1, SIZE[first])]

    def add_up(refs, out):
        v = refs[0][...].astype(F32)
        for r in refs[1:]:
            v = v + r[...].astype(F32)
        out[...] = v.astype(BF16)

    scat1, scat2, scat3 = {}, {}, {}
    for j in (2, 1, 3, 0):
        for part in (2, 0, 1):
            blend_part(part, j)
            scat1[part, j] = scatter1(part, j)

    for j in (2, 1, 3, 0):
        for part in (2, 1, 0):
            second = RS_ORDER[part][1]
            to2 = ahead(second, j)
            piece = t1[part].at[to2]
            add_up(gather1(part, j), piece)
            if j > 0:
                scat2[part, j] = remote(
                    piece, r2[part].at[me[second]], rs2_send.at[part, j], rs2_recv.at[part, j], device(second, j)
                )
                scat2[part, j].start()

    for part in (1, 0, 2):
        second, third = RS_ORDER[part][1:]
        refs = [t1[part].at[me[second]]]
        for j in (2, 1, 3):
            scat2[part, j].wait()
            refs.append(r2[part].at[back(second, j)])
        add_up(refs, t2[part])
        scat3[part] = start([
            remote(t2[part].at[ahead(third, k)], r3[part].at[me[third]], rs3_send.at[part, k], rs3_recv.at[part, k],
                   device(third, k))
            for k in range(1, SIZE[third])
        ])

    col = lax.broadcasted_iota(jnp.int32, (GROUPS, LANES), 1)
    mbuf[...] = sum(jnp.where(col == k, margins[k], 0.0) for k in range(PAIRS))
    mar_ref[...] = mbuf[pl.ds(grp, 1), :][:, 0:PAIRS]
    loss_ref[...] = jnp.sum(loss, axis=0, keepdims=True) * (1.0 / (GROUPS * PAIRS))

    for part in range(3):
        third = RS_ORDER[part][2]
        wait(scat3[part])
        v = t2[part][me[third]].astype(F32)
        for k in range(1, SIZE[third]):
            v = v + r3[part][back(third, k)].astype(F32)
        fbuf[pl.ds(part_at[part], PART_ROWS[part]), :] = v
    mine = fbuf.at[pl.ds(own_at, 64), :]
    swap = remote(mine, mine, fin_send, fin_recv, partner)
    swap.start()
    swap.wait()

    own_inv = invs[pl.ds(me["y"], 1), :]
    own_dot = dotb[pl.ds(me["y"], 1), :]
    own_gain = gainb[pl.ds(pl.multiple_of(sec * BLK, BLK), BLK), :]
    own_hidden = g[me["y"], me["x"], me["z"]].astype(F32)
    result = own_gain * own_inv * fbuf[...] - own_hidden * (own_dot * own_inv * own_inv * (1.0 / D))
    result = jnp.concatenate([result, jnp.zeros((2 * LANES - BLK, LANES), F32)], axis=0)
    flipped = jnp.transpose(result)
    out_ref[...] = jnp.where(core == 0, flipped[0:64, 0:BLK], flipped[64:128, 0:BLK])


def per_device(hidden, norm_gain, weight, targets, segment_ids, pairing, ref_logp):
    vmem = pl.BlockSpec(memory_space=pltpu.VMEM)
    hbm = pl.BlockSpec(memory_space=pl.ANY)
    dma = pltpu.SemaphoreType.DMA
    V = pltpu.VMEM
    grad, margins, loss = pl.pallas_call(
        kernel,
        out_shape=(
            jax.ShapeDtypeStruct((64, BLK), F32),
            jax.ShapeDtypeStruct((1, PAIRS), F32),
            jax.ShapeDtypeStruct((1, 1), F32),
        ),
        in_specs=[hbm] * 7,
        out_specs=(vmem, vmem, vmem),
        scratch_shapes=[
            V((D // LANES, LANES), F32),
            V((GROUPS, 64), jnp.int32),
            V((GROUPS, 64), jnp.int32),
            V((GROUPS, GROUPS), jnp.int32),
            V((GROUPS, GROUPS), F32),
            V((VOC, D), BF16),
            V((NX, NZ, BLK, VPAD), BF16),
            V((NX, NZ, 80, VPAD), BF16),
            V((NY, NX, NZ, BLK, LANES), BF16),
            V((NZ * BLK, TOK), BF16),
            V((VPAD, TOK), F32),
            V((VPAD, TOK), BF16),
            V((VPAD, TOK), BF16),
            V((VPAD, TOK), BF16),
            V((VPAD, TOK), BF16),
            V((D, LANES), F32),
            V((2, 64, BLK), BF16),
            V((8, LANES), F32),
            V((NX, NZ * 32, TOK), F32),
            V((NX, NZ * 32, TOK), F32),
            V((NX, NZ * 16, TOK), F32),
            V((NX, NZ * 32, TOK), BF16),
            V((NX, NZ * 32, TOK), BF16),
            V((NX, NZ * 16, TOK), BF16),
            V((NY, NX, NZ, 32, LANES), BF16),
            V((NX, NY, NZ, 32, LANES), BF16),
            V((NX, NZ, NY, 16, LANES), BF16),
            V((NY, NX, NZ, 32, LANES), BF16),
            V((NX, NY, NZ, 32, LANES), BF16),
            V((NZ, NX, NY, 16, LANES), BF16),
            V((NX, NZ, 32, LANES), BF16),
            V((NY, NZ, 32, LANES), BF16),
            V((NX, NY, 16, LANES), BF16),
            V((NX, NZ, 32, LANES), BF16),
            V((NY, NZ, 32, LANES), BF16),
            V((NX, NY, 16, LANES), BF16),
            V((NZ, 32, LANES), BF16),
            V((NZ, 32, LANES), BF16),
            V((NY, 16, LANES), BF16),
            V((NZ, 32, LANES), BF16),
            V((NZ, 32, LANES), BF16),
            V((NY, 16, LANES), BF16),
            V((BLK, LANES), F32),
            V((NZ, 16, LANES), F32),
            V((NX, 16, LANES), F32),
            V((NY, 16, LANES), F32),
            V((2, 16, LANES), F32),
            V((NZ, 8, LANES), F32),
            V((NX, 8, LANES), F32),
            V((NY, 8, LANES), F32),
            V((8, LANES), F32),
            V((8, LANES), F32),
            V((8, LANES), F32),
            dma((6,)),
            dma((NX,)),
            dma, dma,
            dma((2, NZ)), dma((2, NZ)),
            dma((3, 4)), dma((3, 4)),
            dma((3, 4, NZ)), dma((3, 4, NZ)),
            dma((2, 4, 4)), dma((2, 4, 4)),
            dma((2,)), dma((2,)),
            dma((4,)), dma((4,)),
            dma((4, NZ)), dma((4, NZ)),
            dma((3, NZ)), dma((3, NZ)),
            dma((3, 4, NZ)), dma((3, 4, NZ)),
            dma((3, 4)), dma((3, 4)),
            dma((3, NZ)), dma((3, NZ)),
            dma, dma,
        ],
        compiler_params=pltpu.CompilerParams(
            collective_id=0, has_side_effects=True, vmem_limit_bytes=62 * 2**20
        ),
        name="dpo_output_layer",
    )(
        hidden,
        norm_gain.reshape(D // LANES, LANES),
        weight,
        targets,
        segment_ids,
        pairing,
        ref_logp,
    )
    return (grad, margins, loss.reshape(()))


def solution(mesh):
    in_specs = (P("dp", "section"), P(), P(("section", "dp"), None), P(), P(), P(), P())
    out_specs = (P("dp", "section"), P("dp", None), P())
    return jax.shard_map(
        per_device, mesh=mesh, in_specs=in_specs, out_specs=out_specs, check_vma=False
    )
```

```python
import jax
import jax.numpy as jnp
from jax import lax
from jax.experimental import pallas as pl
from jax.experimental.pallas import tpu as pltpu
from jax.sharding import PartitionSpec as P

SOFTCAP = 30.0
DPO_BETA = 0.5
LOSS_SCALE = 65536.0
EPSILON = 1e-06
MESH = pl.DeviceIdType.MESH

NX, NY, NZ = 4, 4, 8
D = 4608
BLK = 144
TOK = 512
LANES = 128
VOC = 1000
VPAD = 1024
V_ALL = 256000
GROUPS = 8
PAIRS = 4

F32 = jnp.float32
BF16 = jnp.bfloat16

SIZE = {"x": NX, "y": NY, "z": NZ}
AG_ORDER = (("z", "x", "y"), ("z", "y", "x"), ("y", "x", "z"))
OWN = 64
MID = 16
RS_ORDER = (("y", "x", "z"), ("x", "y", "z"), ("z", "x", "y"))
PART_ROWS = (32, 32, 16)
PART_AT = (0, 32, 64)


def kernel(
    hid_hbm, gain_hbm, w_hbm, tgt_hbm, seg_hbm, pair_hbm, ref_hbm,
    out_ref, mar_ref, loss_ref,
    gain_ref, tgt_ref, seg_ref, pair_ref, ref_ref,
    w, wt, wtp, g, n, acc, hot, hotp, dl, dlp, gainb, hbuf, invs,
    u0, u1, u2, a0, a1, a2,
    s0, s1, s2, r01, r11, r21, t01, t11, t21, r02, r12, r22, t02, t12, t22, r03, r13, r23,
    fbuf, arz, arx, ary, arc, sqz, sqx, sqy, coef, dotb, mbuf,
    in_sem, w_sem, core_send, core_recv, ag1_send, ag1_recv, ag2_send, ag2_recv, ag3_send, ag3_recv, fw_send, fw_recv,
    wt_send, wt_recv, dl_send, dl_recv, ar_send, ar_recv, sq_send, sq_recv,
    rs1_send, rs1_recv, rs2_send, rs2_recv, rs3_send, rs3_recv, fin_send, fin_recv,
):
    sec = lax.axis_index("section")
    grp = lax.axis_index("dp")
    me = {"x": sec // NZ, "z": sec % NZ, "y": grp // 2}
    core = grp % 2
    other = 1 - core

    def device(axis, k):
        at = dict(me)
        at[axis] = ahead(axis, k)
        return (at["x"] * NZ + at["z"], at["y"] * 2 + core)

    partner = (sec, me["y"] * 2 + other)

    def ahead(axis, k):
        return lax.rem(me[axis] + k, SIZE[axis])

    def back(axis, k):
        return lax.rem(me[axis] + (SIZE[axis] - k), SIZE[axis])

    def remote(src, dst, ssem, rsem, dev):
        return pltpu.make_async_remote_copy(
            src_ref=src, dst_ref=dst, send_sem=ssem, recv_sem=rsem, device_id=dev, device_id_type=MESH
        )

    def start(copies):
        for c in copies:
            c.start()
        return copies

    def wait(copies):
        for c in copies:
            c.wait()

    cut = NZ * BLK
    small = ((hid_hbm, hbuf.at[core]), (gain_hbm, gain_ref), (tgt_hbm, tgt_ref), (seg_hbm, seg_ref),
             (pair_hbm, pair_ref), (ref_hbm, ref_ref))
    in_copies = start([pltpu.make_async_copy(src, dst, in_sem.at[i]) for i, (src, dst) in enumerate(small)])
    w_copies = start([
        pltpu.make_async_copy(w_hbm.at[:, pl.ds(x * cut, cut)], w.at[:, pl.ds(x * cut, cut)], w_sem.at[x])
        for x in range(NX)
    ])

    barrier = pltpu.get_barrier_semaphore()
    pl.semaphore_signal(barrier, inc=1, device_id=partner, device_id_type=MESH)
    for axis in "xyz":
        for k in range(1, SIZE[axis]):
            pl.semaphore_signal(barrier, inc=1, device_id=device(axis, k), device_id_type=MESH)
    pl.semaphore_wait(barrier, 1 + NX + NY + NZ - 3)

    in_copies[0].wait()
    swap = remote(hbuf.at[core], hbuf.at[core], core_send, core_recv, partner)
    swap.start()
    wait(in_copies[1:])
    swap.wait()
    both = jnp.concatenate([hbuf[0], hbuf[1]], axis=0).astype(F32)
    both = jnp.concatenate([both, jnp.zeros((LANES, 2 * LANES - BLK), F32)], axis=1)
    own_block = jnp.transpose(both)[:BLK]
    own_bits = own_block.astype(BF16)
    own_at = pl.multiple_of(80 * core, 16)
    g[me["y"], me["x"], me["z"], pl.ds(own_at, 64), :] = jnp.where(core == 0, own_bits[0:64], own_bits[80:144])
    g[me["y"], me["x"], me["z"], 64:80, :] = own_bits[64:80]

    part_at = (own_at, pl.multiple_of(80 * core + 32, 16), OWN)

    def g_slice(at, row, rows):
        idx = [at[a] if a in at else pl.ds(0, SIZE[a]) for a in ("y", "x", "z")]
        return g.at[idx[0], idx[1], idx[2], pl.ds(row, rows), :]

    def ag_first(i, axis, row, rows):
        piece = g_slice(me, row, rows)
        return [
            remote(piece, piece, ag1_send.at[i, k], ag1_recv.at[i, k], device(axis, k)) for k in range(1, SIZE[axis])
        ]

    def ag_second(part):
        first, axis, _ = AG_ORDER[part]
        piece = g_slice({a: me[a] for a in me if a != first}, part_at[part], PART_ROWS[part])
        return [
            remote(piece, piece, ag2_send.at[part, k], ag2_recv.at[part, k], device(axis, k)) for k in range(1, 4)
        ]

    def ag_last(part, j):
        _, second, third = AG_ORDER[part]
        piece = g_slice({second: back(second, j), third: me[third]}, part_at[part], PART_ROWS[part])
        return [
            remote(piece, piece, ag3_send.at[part, j, k], ag3_recv.at[part, j, k], device(third, k))
            for k in range(1, SIZE[third])
        ]

    forwards = {}

    def forward(part, j, k):
        _, second, third = AG_ORDER[part]
        piece = g_slice({second: back(second, j), third: back(third, k)}, part_at[part], PART_ROWS[part])
        c = remote(piece, piece, fw_send.at[part, j, k], fw_recv.at[part, j, k], partner)
        c.start()
        forwards[part, j, k] = c

    def sum_copies(buf, axis, ssem, rsem, stage):
        if axis == "c":
            piece = buf.at[core]
            return [remote(piece, piece, ssem.at[stage, 0], rsem.at[stage, 0], partner)]
        piece = buf.at[me[axis]]
        return [
            remote(piece, piece, ssem.at[stage, k], rsem.at[stage, k], device(axis, k)) for k in range(1, SIZE[axis])
        ]

    def sum_start(value, buf, axis, ssem, rsem, stage):
        buf[core if axis == "c" else me[axis]] = value
        return start(sum_copies(buf, axis, ssem, rsem, stage))

    def sum_end(copies, buf):
        wait(copies)
        return jnp.sum(buf[...], axis=0)

    stage1 = start(ag_first(0, "z", own_at, OWN))
    mid1 = start(ag_first(1, "y", OWN, MID))
    squares = jnp.sum((own_block * own_block).reshape(BLK // 8, 8, LANES), axis=0)
    sq = sum_start(squares, sqz, "z", sq_send, sq_recv, 0)

    def transpose_weight(x):
        w_copies[x].wait()
        for i in range(cut // LANES):
            cols = w[:, pl.ds(x * cut + i * LANES, LANES)].astype(F32)
            cols = jnp.concatenate([cols, jnp.zeros((VPAD - VOC, LANES), F32)], axis=0)
            flipped = jnp.transpose(cols).astype(BF16)
            row = i * LANES
            while row < (i + 1) * LANES:
                z, off = row // BLK, row % BLK
                count = min(BLK - off, (i + 1) * LANES - row)
                wt[x, z, off:off + count, :] = flipped[row - i * LANES:row - i * LANES + count]
                row += count

    def gain_rows(i, carry):
        for q in range(4):
            row = 1.0 + gain_ref[pl.ds(4 * i + q, 1), :]
            gainb[pl.ds(pl.multiple_of((4 * i + q) * LANES, LANES), LANES), :] = jnp.transpose(
                jnp.broadcast_to(row, (LANES, LANES))
            )
        return carry

    stage2, stage3 = {}, {}

    def first_done(p):
        stage2[p] = start(ag_second(p))
        stage3[p, 0] = start(ag_last(p, 0))
        if p < 2:
            forward(p, 0, 0)

    transpose_weight(0)
    transpose_weight(1)
    wait(mid1)
    first_done(2)
    transpose_weight(2)
    transpose_weight(3)
    wait(stage1)
    first_done(0)
    first_done(1)
    sq = sum_start(sum_end(sq, sqz), sqx, "x", sq_send, sq_recv, 1)

    tile = 128
    vocab_start = (sec * 2 * NY + grp) * VOC
    other_start = (sec * 2 * NY + me["y"] * 2 + other) * VOC
    half = lax.broadcasted_iota(jnp.int32, (1, LANES), 1) < 64
    tgt = jnp.concatenate([tgt_ref[...], tgt_ref[...]], axis=1)
    targets = jnp.concatenate(
        [jnp.where(half, tgt[2 * y:2 * y + 1], tgt[2 * y + 1:2 * y + 2]) for y in range(NY)], axis=1
    )

    def row_ids(i):
        return i * tile + lax.broadcasted_iota(jnp.int32, (tile, TOK), 0)

    def hot_tile(i, carry):
        at = pl.ds(pl.multiple_of(i * tile, tile), tile)
        ids = row_ids(i)
        ids = jnp.where(ids < VOC, ids, -2 * V_ALL)
        hot[at, :] = (ids + vocab_start == targets).astype(F32).astype(BF16)
        hotp[at, :] = (ids + other_start == targets).astype(F32).astype(BF16)
        return carry


    def rows_product(part, xs, mine, right, out, add):
        rows = PART_ROWS[part]
        ref, at = (wt, part_at[part]) if mine else (wtp, PART_AT[part])

        def body(i, carry):
            xat = pl.ds(i * xs, xs)
            left = ref[xat, :, pl.ds(at, rows), :].reshape(xs * NZ * rows, VPAD)
            t = jnp.dot(left, right[...], preferred_element_type=F32).reshape(xs, NZ * rows, TOK)
            if add:
                t = t + out[xat].astype(F32)
            out[xat] = t.astype(out.dtype)
            return carry

        lax.fori_loop(0, NX // xs, body, 0)

    def product(mine, right, outs, add):
        for part, xs in ((0, 2), (1, 2), (2, 4)):
            rows_product(part, xs, mine, right, outs[part], add)

    for j in (1, 3, 2):
        for p in (2, 0, 1):
            stage2[p][j - 1].wait()
            stage3[p, j] = start(ag_last(p, j))
            if p < 2:
                forward(p, j, 0)
    sq = sum_start(sum_end(sq, sqx), sqy, "y", sq_send, sq_recv, 2)
    lax.fori_loop(0, D // LANES // 4, gain_rows, 0)
    lax.fori_loop(0, VPAD // tile, hot_tile, 0)

    wait(sq)
    mean_sq = jnp.concatenate([jnp.sum(sqy[y], axis=0, keepdims=True) for y in range(NY)], axis=0) / D
    invs[0:NY, :] = lax.rsqrt(mean_sq + EPSILON)

    def pass_on(j):
        for k in (1, 3, 2):
            stage3[0, j][k - 1].wait()
            forward(0, j, k)
        if j > 0:
            for jj in (0, 1, 3, 2):
                stage3[1, jj][j - 1].wait()
                forward(1, jj, j)

    def logits(j, first):
        wait(stage3[2, j])
        for k in range(4):
            forwards[0, j, k].wait()
            forwards[1, k, j].wait()
        xb = back("x", j)

        def normalize(z, carry):
            rows = pl.ds(pl.multiple_of(z * BLK, BLK), BLK)
            gain = gainb[pl.ds(pl.multiple_of((xb * NZ + z) * BLK, BLK), BLK), :]
            for y in range(NY):
                h = g[y, xb, z].astype(F32)
                n[rows, y * LANES:(y + 1) * LANES] = (h * invs[y:y + 1, :] * gain).astype(BF16)
            return carry

        lax.fori_loop(0, NZ, normalize, 0)
        t = jnp.dot(w[:, pl.ds(pl.multiple_of(xb * cut, LANES), cut)], n[...], preferred_element_type=F32)
        if first:
            acc[0:VOC, :] = t
        else:
            acc[0:VOC, :] += t

    pass_on(0)
    pass_on(1)
    logits(0, True)
    pass_on(3)
    logits(1, False)
    pass_on(2)
    far = pl.multiple_of(80 * other, 16)
    wt_copies = start([
        remote(wt.at[:, :, pl.ds(far, 64), :], wtp.at[:, :, pl.ds(0, 64), :], wt_send.at[0], wt_recv.at[0], partner),
        remote(wt.at[:, :, pl.ds(64, 16), :], wtp.at[:, :, pl.ds(64, 16), :], wt_send.at[1], wt_recv.at[1], partner),
    ])
    logits(3, False)
    logits(2, False)

    def fold(v):
        return jnp.sum(v.reshape(tile // 8, 8, TOK), axis=0)

    def softmax_tile(i, carry):
        tot, pick, dots = carry
        at = pl.ds(pl.multiple_of(i * tile, tile), tile)
        ids = row_ids(i)
        valid = ids < VOC
        raw = acc[at, :]
        th = jnp.tanh(raw * (1.0 / SOFTCAP))
        e = jnp.where(valid, jnp.exp(SOFTCAP * th), 0.0)
        at_target = jnp.logical_and(ids + vocab_start == targets, valid)
        term = jnp.where(jnp.logical_or(at_target, jnp.logical_not(valid)), 0.0, e * (1.0 - th * th)).astype(BF16)
        dl[at, :] = term
        term = term.astype(F32)
        return (
            tot + fold(e),
            pick + fold(jnp.where(at_target, raw, 0.0)),
            dots + fold(jnp.where(term == 0.0, 0.0, term * raw)),
        )

    zero = jnp.zeros((8, TOK), F32)
    carry = (zero, zero, zero)
    dl_copies = []
    for q in range(4):
        carry = lax.fori_loop(2 * q, 2 * q + 2, softmax_tile, carry)
        at = pl.ds(q * 2 * tile, 2 * tile)
        dl_copies += start([remote(dl.at[at, :], dlp.at[at, :], dl_send.at[q], dl_recv.at[q], partner)])

    def to_rows(v):
        v = jnp.sum(v, axis=0, keepdims=True)
        return [v[:, y * LANES:(y + 1) * LANES] for y in range(NY)]

    value = jnp.concatenate(
        to_rows(carry[0]) + to_rows(carry[1]) + to_rows(carry[2]) + [jnp.zeros((NY, LANES), F32)], axis=0
    )
    sums = sum_start(value, arz, "z", ar_send, ar_recv, 0)
    product(True, dl, (u0, u1, u2), False)
    product(True, hot, (a0, a1, a2), False)
    sums = sum_start(sum_end(sums, arz), arx, "x", ar_send, ar_recv, 1)
    wait(wt_copies)
    product(False, hotp, (a0, a1, a2), True)
    sums = sum_start(sum_end(sums, arx), ary, "y", ar_send, ar_recv, 2)
    wait(dl_copies)
    product(False, dlp, (u0, u1, u2), True)
    sums = sum_start(sum_end(sums, ary), arc, "c", ar_send, ar_recv, 3)
    value = sum_end(sums, arc)

    exp_total = value[0:NY]
    target_raw = value[NY:2 * NY]
    dots = value[2 * NY:3 * NY]
    target_th = jnp.tanh(target_raw * (1.0 / SOFTCAP))
    target_capped = SOFTCAP * target_th
    logp = target_capped - jnp.log(exp_total)

    lane = lax.broadcasted_iota(jnp.int32, (GROUPS, LANES), 1)
    group = lax.broadcasted_iota(jnp.int32, (GROUPS, LANES), 0)
    own_half = (lane // 64) == (group % 2)
    seg = jnp.where(own_half, jnp.concatenate([seg_ref[...], seg_ref[...]], axis=1), -1)
    logp = jnp.concatenate([logp[r // 2:r // 2 + 1] for r in range(GROUPS)], axis=0)
    pairing = pair_ref[...]
    ref_logp = ref_ref[...]
    members, counts, adjusted = [], [], []
    for s in range(GROUPS):
        member = (seg == s).astype(F32)
        count = jnp.sum(member, axis=1, keepdims=True)
        members.append(member)
        counts.append(count)
        adjusted.append(jnp.sum(member * logp, axis=1, keepdims=True) / count - ref_logp[:, s:s + 1])
    margins, pulls, hots = [], [], []
    loss = jnp.zeros((GROUPS, 1), F32)
    for k in range(PAIRS):
        signs = [
            (pairing[:, 2 * k:2 * k + 1] == s).astype(F32) - (pairing[:, 2 * k + 1:2 * k + 2] == s).astype(F32)
            for s in range(GROUPS)
        ]
        margin = DPO_BETA * sum(sign * a for sign, a in zip(signs, adjusted))
        loss = loss + jnp.maximum(-margin, 0.0) + jnp.log1p(jnp.exp(-jnp.abs(margin)))
        hots.append(signs)
        margins.append(margin)
        pulls.append(-jax.nn.sigmoid(-margin) * (LOSS_SCALE / (GROUPS * PAIRS)))
    weight_rows = jnp.zeros((GROUPS, LANES), F32)
    for s in range(GROUPS):
        pull = DPO_BETA * sum(hots[k][s] * pulls[k] for k in range(PAIRS)) / counts[s]
        weight_rows = weight_rows + members[s] * pull
    token_weight = jnp.concatenate(
        [weight_rows[2 * y:2 * y + 1] + weight_rows[2 * y + 1:2 * y + 2] for y in range(NY)], axis=0
    )
    inv_total = 1.0 / exp_total
    at_target = token_weight * (1.0 - jnp.exp(target_capped) * inv_total) * (1.0 - target_th * target_th)
    elsewhere = -token_weight * inv_total
    coef[0:NY, :] = at_target
    coef[NY:2 * NY, :] = elsewhere
    dotb[0:NY, :] = jnp.where(at_target == 0.0, 0.0, at_target * target_raw) + elsewhere * dots

    s_bufs, r1, t1, r2 = (s0, s1, s2), (r01, r11, r21), (t01, t11, t21), (r02, r12, r22)
    t2, r3 = (t02, t12, t22), (r03, r13, r23)
    u_bufs, a_bufs = (u0, u1, u2), (a0, a1, a2)

    def blend(part, y, xb):
        rows = PART_ROWS[part]
        at = pl.ds(pl.multiple_of(y * LANES, LANES), LANES)
        v = coef[pl.ds(y, 1), :] * a_bufs[part][xb, :, at].astype(F32)
        v = v + coef[pl.ds(NY + y, 1), :] * u_bufs[part][xb, :, at]
        return v.astype(BF16).reshape(NZ, rows, LANES)

    def blend_part(part, j):
        def body(i, carry):
            if part == 0:
                s0[i, ahead("x", j)] = blend(0, i, ahead("x", j))
            elif part == 1:
                s1[i, ahead("y", j)] = blend(1, ahead("y", j), i)
            else:
                s2[ahead("x", j), :, i] = blend(2, i, ahead("x", j))
            return carry

        lax.fori_loop(0, 4, body, 0)

    def scatter1(part, j):
        first, second, _ = RS_ORDER[part]
        to2 = ahead(second, j)
        copies = []
        for k in range(1, SIZE[first]):
            to1 = ahead(first, k)
            src = s2.at[to2, to1] if part == 2 else s_bufs[part].at[to1, to2]
            copies.append(
                remote(src, r1[part].at[me[first], to2], rs1_send.at[part, j, k], rs1_recv.at[part, j, k],
                       device(first, k))
            )
        return start(copies)

    def gather1(part, j):
        first, second, _ = RS_ORDER[part]
        wait(scat1[part, j])
        to2 = ahead(second, j)
        own = s2.at[to2, me["z"]] if part == 2 else s_bufs[part].at[me[first], to2]
        return [own] + [r1[part].at[back(first, k), to2] for k in range(1, SIZE[first])]

    def add_up(refs, out):
        v = refs[0][...].astype(F32)
        for r in refs[1:]:
            v = v + r[...].astype(F32)
        out[...] = v.astype(BF16)

    scat1, scat2, scat3 = {}, {}, {}
    for j in (2, 1, 3, 0):
        for part in (2, 0, 1):
            blend_part(part, j)
            scat1[part, j] = scatter1(part, j)

    for j in (2, 1, 3, 0):
        for part in (0, 1, 2):
            second = RS_ORDER[part][1]
            to2 = ahead(second, j)
            piece = t1[part].at[to2]
            add_up(gather1(part, j), piece)
            if j > 0:
                scat2[part, j] = remote(
                    piece, r2[part].at[me[second]], rs2_send.at[part, j], rs2_recv.at[part, j], device(second, j)
                )
                scat2[part, j].start()

    for part in (1, 0, 2):
        second, third = RS_ORDER[part][1:]
        refs = [t1[part].at[me[second]]]
        for j in (2, 1, 3):
            scat2[part, j].wait()
            refs.append(r2[part].at[back(second, j)])
        add_up(refs, t2[part])
        scat3[part] = start([
            remote(t2[part].at[ahead(third, k)], r3[part].at[me[third]], rs3_send.at[part, k], rs3_recv.at[part, k],
                   device(third, k))
            for k in range(1, SIZE[third])
        ])

    col = lax.broadcasted_iota(jnp.int32, (GROUPS, LANES), 1)
    mbuf[...] = sum(jnp.where(col == k, margins[k], 0.0) for k in range(PAIRS))
    mar_ref[...] = mbuf[pl.ds(grp, 1), :][:, 0:PAIRS]
    loss_ref[...] = jnp.sum(loss, axis=0, keepdims=True) * (1.0 / (GROUPS * PAIRS))

    for part in range(3):
        third = RS_ORDER[part][2]
        wait(scat3[part])
        v = t2[part][me[third]].astype(F32)
        for k in range(1, SIZE[third]):
            v = v + r3[part][back(third, k)].astype(F32)
        fbuf[pl.ds(part_at[part], PART_ROWS[part]), :] = v
    mine = fbuf.at[pl.ds(own_at, 64), :]
    swap = remote(mine, mine, fin_send, fin_recv, partner)
    swap.start()
    swap.wait()

    own_inv = invs[pl.ds(me["y"], 1), :]
    own_dot = dotb[pl.ds(me["y"], 1), :]
    own_gain = gainb[pl.ds(pl.multiple_of(sec * BLK, BLK), BLK), :]
    own_hidden = g[me["y"], me["x"], me["z"]].astype(F32)
    result = own_gain * own_inv * fbuf[...] - own_hidden * (own_dot * own_inv * own_inv * (1.0 / D))
    result = jnp.concatenate([result, jnp.zeros((2 * LANES - BLK, LANES), F32)], axis=0)
    flipped = jnp.transpose(result)
    out_ref[...] = jnp.where(core == 0, flipped[0:64, 0:BLK], flipped[64:128, 0:BLK])


def per_device(hidden, norm_gain, weight, targets, segment_ids, pairing, ref_logp):
    vmem = pl.BlockSpec(memory_space=pltpu.VMEM)
    hbm = pl.BlockSpec(memory_space=pl.ANY)
    dma = pltpu.SemaphoreType.DMA
    V = pltpu.VMEM
    grad, margins, loss = pl.pallas_call(
        kernel,
        out_shape=(
            jax.ShapeDtypeStruct((64, BLK), F32),
            jax.ShapeDtypeStruct((1, PAIRS), F32),
            jax.ShapeDtypeStruct((1, 1), F32),
        ),
        in_specs=[hbm] * 7,
        out_specs=(vmem, vmem, vmem),
        scratch_shapes=[
            V((D // LANES, LANES), F32),
            V((GROUPS, 64), jnp.int32),
            V((GROUPS, 64), jnp.int32),
            V((GROUPS, GROUPS), jnp.int32),
            V((GROUPS, GROUPS), F32),
            V((VOC, D), BF16),
            V((NX, NZ, BLK, VPAD), BF16),
            V((NX, NZ, 80, VPAD), BF16),
            V((NY, NX, NZ, BLK, LANES), BF16),
            V((NZ * BLK, TOK), BF16),
            V((VPAD, TOK), F32),
            V((VPAD, TOK), BF16),
            V((VPAD, TOK), BF16),
            V((VPAD, TOK), BF16),
            V((VPAD, TOK), BF16),
            V((D, LANES), F32),
            V((2, 64, BLK), BF16),
            V((8, LANES), F32),
            V((NX, NZ * 32, TOK), F32),
            V((NX, NZ * 32, TOK), F32),
            V((NX, NZ * 16, TOK), F32),
            V((NX, NZ * 32, TOK), BF16),
            V((NX, NZ * 32, TOK), BF16),
            V((NX, NZ * 16, TOK), BF16),
            V((NY, NX, NZ, 32, LANES), BF16),
            V((NX, NY, NZ, 32, LANES), BF16),
            V((NX, NZ, NY, 16, LANES), BF16),
            V((NY, NX, NZ, 32, LANES), BF16),
            V((NX, NY, NZ, 32, LANES), BF16),
            V((NZ, NX, NY, 16, LANES), BF16),
            V((NX, NZ, 32, LANES), BF16),
            V((NY, NZ, 32, LANES), BF16),
            V((NX, NY, 16, LANES), BF16),
            V((NX, NZ, 32, LANES), BF16),
            V((NY, NZ, 32, LANES), BF16),
            V((NX, NY, 16, LANES), BF16),
            V((NZ, 32, LANES), BF16),
            V((NZ, 32, LANES), BF16),
            V((NY, 16, LANES), BF16),
            V((NZ, 32, LANES), BF16),
            V((NZ, 32, LANES), BF16),
            V((NY, 16, LANES), BF16),
            V((BLK, LANES), F32),
            V((NZ, 16, LANES), F32),
            V((NX, 16, LANES), F32),
            V((NY, 16, LANES), F32),
            V((2, 16, LANES), F32),
            V((NZ, 8, LANES), F32),
            V((NX, 8, LANES), F32),
            V((NY, 8, LANES), F32),
            V((8, LANES), F32),
            V((8, LANES), F32),
            V((8, LANES), F32),
            dma((6,)),
            dma((NX,)),
            dma, dma,
            dma((2, NZ)), dma((2, NZ)),
            dma((3, 4)), dma((3, 4)),
            dma((3, 4, NZ)), dma((3, 4, NZ)),
            dma((2, 4, 4)), dma((2, 4, 4)),
            dma((2,)), dma((2,)),
            dma((4,)), dma((4,)),
            dma((4, NZ)), dma((4, NZ)),
            dma((3, NZ)), dma((3, NZ)),
            dma((3, 4, NZ)), dma((3, 4, NZ)),
            dma((3, 4)), dma((3, 4)),
            dma((3, NZ)), dma((3, NZ)),
            dma, dma,
        ],
        compiler_params=pltpu.CompilerParams(
            collective_id=0, has_side_effects=True, vmem_limit_bytes=62 * 2**20
        ),
        name="dpo_output_layer",
    )(
        hidden,
        norm_gain.reshape(D // LANES, LANES),
        weight,
        targets,
        segment_ids,
        pairing,
        ref_logp,
    )
    return (grad, margins, loss.reshape(()))


def solution(mesh):
    in_specs = (P("dp", "section"), P(), P(("section", "dp"), None), P(), P(), P(), P())
    out_specs = (P("dp", "section"), P("dp", None), P())
    return jax.shard_map(
        per_device, mesh=mesh, in_specs=in_specs, out_specs=out_specs, check_vma=False
    )
```
